256 devices in a mesh: replica: 16 (over z, core), fsdp: 4 (over y), tensor: 4 (over x).
Axes of the slice: x: 4, y: 4, z: 8, core: 2. Of those that a mesh axis runs over, the one named last changes fastest.
Arguments:
- activations: bfloat16 [32768, 8192], P(('replica', 'fsdp', 'tensor')), may hold values from -6 to 6
- cotangent: bfloat16 [32768, 2048], P(('replica', 'fsdp'), 'tensor'), may hold values from -0.625 to 0.625
- momentum: float32 [16, 8192, 2048], P('replica', 'fsdp', 'tensor'), may hold values from -6 to 6
- band_index: int32 [16, 128, 32, 16], P('replica', 'fsdp', 'tensor'), may hold values from 0 to 975, as said below
Outputs:
- new_momentum: float32 [16, 8192, 2048], P('replica', 'fsdp', 'tensor')
- update: bfloat16 [8192, 2048], P('fsdp', 'tensor')
The draws below stay inside these ranges and needn't reach their ends.
Inputs may be any that keep to these rules, and one draw needn't show every extreme that they name: `band_index`: within each block the 16 indices of a replica are distinct, and each is k1 * 64 + k2 with k1 and k2 below 16.
All inputs are finite; a program needn't handle non-finite values.
Results may differ from the reference program's by a relative error of at most 0.0011.
Values may be sent and summed in bfloat16 or wider, within the bound.
No kernel may reach another device: no remote copies, remote signals or barrier semaphores. Data moves between devices by JAX's collectives and lax.ppermute only.
A program may use at most 128 MiB of HBM per device.

```python
import math
import jax
import jax.numpy as jnp
from jax import lax

D = 8192
TOK_DEV = 128
SPAN = 64
LOW = 16
BAND = 16
KV = 2048
REPLICAS = 16
TOKENS = 32768
ROW_SPANS = 128
COL_SPANS = 32
N_TENSOR = 4


def draw_band_index(key, part):
    key = jax.random.fold_in(key, 7)
    scores = jax.random.randint(key, (REPLICAS, ROW_SPANS, COL_SPANS, LOW * LOW), 0, 1 << 20, dtype=jnp.int32)
    chosen = jnp.argsort(scores, axis=-1, stable=True)[..., :BAND].astype(jnp.int32)
    return (chosen // LOW * SPAN + chosen % LOW).astype(jnp.int32)


def level_of(rng, shape, split, least, largest):
    def one(dim, blocks):
        steps = jax.random.uniform(jax.random.fold_in(jax.random.fold_in(rng, 6), dim), (blocks,), jnp.float32, least / len(split), largest / len(split))
        return jnp.repeat(jnp.exp(steps), shape[dim] // blocks).reshape((-1,) + (1,) * (len(shape) - dim - 1))

    loudness = one(*split[0])
    for cut in split[1:]:
        loudness = loudness * one(*cut)
    return loudness


def scatter_about(stream_key, dims, width, bound, shards=(), held_as=jnp.bfloat16):
    result = jax.random.normal(stream_key, dims, jnp.float32) * width
    if len(shards) > 0:
        result = level_of(stream_key, dims, shards, -0.22, 0.18) * result
    return jnp.clip(result, min=-bound, max=bound).astype(held_as)


def setup_inputs(seed: int = 0) -> dict:
    key_list = jax.random.split(jax.random.key(seed), 5)
    activations = scatter_about(key_list[0], (TOKENS, D), 1.0, 6.0, ((0, 256),))
    cotangent = scatter_about(key_list[1], (TOKENS, KV), ((TOK_DEV * N_TENSOR) ** -0.5), 0.625, ((0, 64), (1, 4)))
    momentum = scatter_about(key_list[2], (REPLICAS, D, KV), 1.0, 6.0, ((0, 16), (1, 4), (2, 4)), jnp.float32)
    band_index = draw_band_index(jax.random.fold_in(key_list[4], 71), 0)
    return {"activations": activations, "cotangent": cotangent, "momentum": momentum, "band_index": band_index}


decay_rate = 0.999

def cosine_table(count):
    frequency = jnp.arange(count, dtype=jnp.float32)[:, None]
    position = jnp.arange(SPAN, dtype=jnp.float32)[None, :]
    raw_table = jnp.cos(math.pi * (2.0 * position + 1.0) * frequency / (2.0 * SPAN))
    weight = jnp.where(frequency == 0, math.sqrt(1.0 / SPAN), math.sqrt(2.0 / SPAN))
    return raw_table * weight

def reference(activations, cotangent, momentum, band_index):
    cosine_rows = cosine_table(SPAN)
    group_rows = TOKENS // REPLICAS
    inputs = activations.reshape(REPLICAS, group_rows, D)
    grads_out = cotangent.reshape(REPLICAS, group_rows, KV)
    row_ids = jnp.arange(ROW_SPANS, dtype=jnp.int32)[:, None, None]
    col_ids = jnp.arange(COL_SPANS, dtype=jnp.int32)[None, :, None]

    def one_replica(operands):
        inputs_r, grads_r, momentum_r, index_r = operands
        gradient = jnp.dot(inputs_r.T, grads_r, preferred_element_type=jnp.float32)
        blended = decay_rate * momentum_r + gradient
        blocks = blended.reshape(ROW_SPANS, SPAN, COL_SPANS, SPAN)
        coeffs = jnp.einsum('ki,aibj,lj->abkl', cosine_rows, blocks, cosine_rows, precision=lax.Precision.HIGHEST)
        flat_coeffs = coeffs.reshape(ROW_SPANS, COL_SPANS, SPAN * SPAN)
        values = jnp.take_along_axis(flat_coeffs, index_r, axis=-1)
        kept_coeffs = jnp.zeros_like(flat_coeffs).at[row_ids, col_ids, index_r].set(values)
        removed = jnp.einsum('ki,abkl,lj->aibj', cosine_rows, kept_coeffs.reshape(ROW_SPANS, COL_SPANS, SPAN, SPAN), cosine_rows, precision=lax.Precision.HIGHEST)
        return (blended - removed.reshape(D, KV), values)
    new_momentum, values = lax.map(one_replica, (inputs, grads_out, momentum, band_index))
    combined = jnp.zeros((ROW_SPANS, COL_SPANS, SPAN * SPAN), jnp.float32)
    combined = combined.at[row_ids[None], col_ids[None], band_index].add(values)
    spatial = jnp.einsum('ki,abkl,lj->aibj', cosine_rows, combined.reshape(ROW_SPANS, COL_SPANS, SPAN, SPAN), cosine_rows, precision=lax.Precision.HIGHEST)
    return (new_momentum, spatial.reshape(D, KV).astype(jnp.bfloat16))
```

```python
import functools

import jax
import jax.numpy as jnp
import ml_dtypes
import numpy as np
from jax import lax
from jax.experimental import pallas as pl
from jax.experimental.pallas import tpu as pltpu
from jax.sharding import PartitionSpec as P

SPAN = 64
LOW = 16
TILE = 256
DECAY = 0.999
VMEM_LIMIT = 40 * 1024 * 1024


def split_table(table):
    high = table.astype(ml_dtypes.bfloat16)
    low = (table - high.astype(np.float64)).astype(ml_dtypes.bfloat16)
    return high, low


def tables(cols):
    frequency = np.arange(LOW)[:, None]
    position = np.arange(SPAN)[None, :]
    cosine = np.cos(np.pi * (2.0 * position + 1.0) * frequency / (2.0 * SPAN))
    cosine = cosine * np.where(frequency == 0, np.sqrt(1.0 / SPAN), np.sqrt(2.0 / SPAN))
    down_high, down_low = split_table(np.kron(np.eye(TILE // SPAN), cosine))
    across_high, across_low = split_table(np.kron(np.eye(cols // SPAN), cosine))
    return {
        "rows": np.concatenate([down_high, down_low], 0),
        "cols_high": np.ascontiguousarray(across_high.T),
        "cols_low": np.ascontiguousarray(across_low.T),
        "back_high": across_high,
        "back_low": across_low,
        "back_rows": np.concatenate([down_high.T, down_high.T, down_low.T], 1),
    }


def halves(x):
    high = x.astype(jnp.bfloat16)
    return high, (x - high.astype(jnp.float32)).astype(jnp.bfloat16)


def dot(a, b):
    return jnp.dot(a, b, preferred_element_type=jnp.float32)


def times_table(x, high, low):
    rows = x.shape[0]
    x_high, x_low = halves(x)
    both = dot(jnp.concatenate([x_high, x_low], 0), high)
    return both[:rows] + both[rows:] + dot(x_high, low)


def forward(x, rows_ref, cols_high_ref, cols_low_ref):
    x_high, x_low = halves(x)
    count = rows_ref.shape[0] // 2
    both = dot(rows_ref[...], x_high)
    down = both[:count] + both[count:] + dot(rows_ref[:count, :], x_low)
    return times_table(down, cols_high_ref[...], cols_low_ref[...])


def backward(coefficients, back_high_ref, back_low_ref, back_rows_ref):
    across = times_table(coefficients, back_high_ref[...], back_low_ref[...])
    high, low = halves(across)
    return dot(back_rows_ref[...], jnp.concatenate([high, low, high], 0))


def order_kernel(tensor_ref, *refs):
    parts, out_ref = refs[:4], refs[4]
    for shift in range(4):
        start = lax.rem(tensor_ref[0] + 4 - shift, 4) * 128
        for d in range(4):
            out_ref[pl.ds((shift * 4 + d) * 128, 128), :] = parts[d][pl.ds(pl.multiple_of(start, 128), 128), :]


def chunk_kernel(splits, first, *refs):
    own = refs[:4]
    others = refs[4 : 4 + 4 * splits]
    refs = refs[4 + 4 * splits :]
    cot_ref, momentum_ref, mask_ref, rows_ref, ch_ref, cl_ref, bh_ref, bl_ref, br_ref = refs[:9]
    new_ref, kept_ref, lhs = refs[-3:]
    step = pl.program_id(0)
    for shift in range(4):
        lhs[pl.ds(shift * 512, 128), :] = own[shift][...]
        if splits == 1:
            lhs[pl.ds(shift * 512 + 128, 384), :] = others[shift][...]
        else:
            for part in range(splits):

                @pl.when(step == part)
                def _():
                    lhs[pl.ds(shift * 512 + 128, 384), :] = others[part * 4 + shift][...]

    gradient = lax.dot_general(
        lhs[...], cot_ref[...], (((0,), (0,)), ((), ())), preferred_element_type=jnp.float32
    )
    blended = DECAY * momentum_ref[...] + gradient
    kept = forward(blended, rows_ref, ch_ref, cl_ref) * mask_ref[...]
    kept_ref[...] = kept
    new_ref[...] = blended - backward(kept, bh_ref, bl_ref, br_ref)


def whole(shape):
    return pl.BlockSpec(shape, lambda i: (0,) * len(shape))


def chunk(c, own, others, cot, momentum, mask, consts, previous):
    rows, cols = momentum.shape
    splits = len(others)
    steps = 2
    low_rows = TILE // SPAN * LOW
    low_cols = cols // SPAN * LOW
    in_specs = [pl.BlockSpec((128, TILE), lambda i: (0, 2 * c + i))] * 4
    if splits == 1:
        in_specs += [pl.BlockSpec((384, TILE), lambda i: (0, i))] * 4
    else:
        in_specs += [whole((384, TILE))] * (4 * splits)
    in_specs += [
        whole(cot.shape),
        pl.BlockSpec((TILE, cols), lambda i: (2 * c + i, 0)),
        pl.BlockSpec((low_rows, low_cols), lambda i: (2 * c + i, 0)),
    ]
    in_specs += [whole(x.shape) for x in consts]
    args = [*own, *[x for part in others for x in part], cot, momentum, mask, *consts]
    aliases = {}
    if previous is not None:
        in_specs.append(pl.BlockSpec(memory_space=pl.ANY))
        args.append(previous)
        aliases = {len(args) - 1: 0}
    return pl.pallas_call(
        functools.partial(chunk_kernel, splits, previous is None),
        grid=(steps,),
        in_specs=in_specs,
        out_specs=[
            pl.BlockSpec((TILE, cols), lambda i: (2 * c + i, 0)),
            pl.BlockSpec((low_rows, low_cols), lambda i: (i, 0)),
        ],
        out_shape=[
            jax.ShapeDtypeStruct((rows, cols), jnp.float32),
            jax.ShapeDtypeStruct((steps * low_rows, low_cols), jnp.float32),
        ],
        scratch_shapes=[pltpu.VMEM((2048, TILE), jnp.bfloat16)],
        input_output_aliases=aliases,
        compiler_params=pltpu.CompilerParams(vmem_limit_bytes=VMEM_LIMIT),
        cost_estimate=pl.CostEstimate(
            flops=2 * 2048 * 512 * cols * 2, bytes_accessed=6 * 2**20, transcendentals=0
        ),
        name=f"chunk{c}",
    )(*args)


def update_kernel(coefficients_ref, bh_ref, bl_ref, br_ref, *refs):
    out_ref = refs[-1]
    out_ref[...] = backward(coefficients_ref[...], bh_ref, bl_ref, br_ref).astype(out_ref.dtype)


def spread(start, coefficients, shape, consts, previous):
    rows, cols = shape
    low_rows = TILE // SPAN * LOW
    steps = coefficients.shape[0] // low_rows
    in_specs = [pl.BlockSpec((low_rows, coefficients.shape[1]), lambda i: (i, 0))]
    in_specs += [whole(x.shape) for x in consts]
    args = [coefficients, *consts]
    aliases = {}
    if previous is not None:
        in_specs.append(pl.BlockSpec(memory_space=pl.ANY))
        args.append(previous)
        aliases = {len(args) - 1: 0}
    return pl.pallas_call(
        update_kernel,
        grid=(steps,),
        in_specs=in_specs,
        out_specs=pl.BlockSpec((TILE, cols), lambda i: (start + i, 0)),
        out_shape=jax.ShapeDtypeStruct((rows, cols), jnp.bfloat16),
        input_output_aliases=aliases,
        compiler_params=pltpu.CompilerParams(vmem_limit_bytes=VMEM_LIMIT),
        cost_estimate=pl.CostEstimate(flops=steps * 10**8, bytes_accessed=steps * 2**18, transcendentals=0),
        name=f"spread{start}",
    )(*args)


def shifted(x, axis, by, count):
    return lax.ppermute(x, axis, [(i, (i + by) % count) for i in range(count)])


def around(x, right):
    plus = shifted(x, "tensor", 1, 4)
    minus = shifted(x, "tensor", -1, 4)
    far = shifted(plus, "tensor", 1, 4) if right else shifted(minus, "tensor", -1, 4)
    return [x, plus, far, minus]


def over_replicas(x):
    for bit in (1, 2, 4, 8):
        x = x + lax.ppermute(x, "replica", [(i, i ^ bit) for i in range(16)])
    return x


def band_mask(band_index, cols):
    span_rows, span_cols, band = band_index.shape
    wide = jnp.repeat(band_index.transpose(2, 0, 1), LOW, axis=2)
    k1 = jnp.arange(LOW, dtype=jnp.int32)[None, :, None]
    k2 = jnp.arange(span_cols * LOW, dtype=jnp.int32)[None, None, :] % LOW
    here = k1 * SPAN + k2
    hit = functools.reduce(jnp.logical_or, [wide[j][:, None, :] == here for j in range(band)])
    return hit.astype(jnp.float32).reshape(span_rows * LOW, span_cols * LOW)


def local(activations, cotangent, momentum, band_index):
    momentum = momentum[0]
    rows, cols = momentum.shape
    fsdp = lax.axis_index("fsdp")
    tensor = lax.axis_index("tensor")
    table = tables(cols)
    forward_consts = [jnp.asarray(table[k]) for k in ("rows", "cols_high", "cols_low")]
    backward_consts = [jnp.asarray(table[k]) for k in ("back_high", "back_low", "back_rows")]
    consts = forward_consts + backward_consts

    def columns(d, start, width):
        owner = lax.rem(fsdp + d, 4)
        return lax.dynamic_slice(activations, (0, owner * rows + start), (128, width))

    own = around(columns(0, 0, rows), True)
    early = [shifted(columns(d, 0, 512), "fsdp", d, 4) for d in (1, 2, 3)]
    late = [shifted(columns(d, 512, 1536), "fsdp", d, 4) for d in (1, 2, 3)]
    cot_plus = shifted(cotangent, "fsdp", 1, 4)
    cot_minus = shifted(cotangent, "fsdp", -1, 4)
    cot_far = shifted(cot_plus, "fsdp", 1, 4)

    def stacked(parts, start, width):
        return jnp.concatenate([p[:, start : start + width] for p in parts], 0)

    others = [
        [around(stacked(early, 0, 512), False)],
        [around(stacked(late, 0, 512), True)],
        [around(stacked(late, 512, 512), False)],
        [around(stacked(late, 1024, 256), True), around(stacked(late, 1280, 256), False)],
    ]

    cot = pl.pallas_call(
        order_kernel,
        in_specs=[pl.BlockSpec(memory_space=pltpu.SMEM)] + [pl.BlockSpec(memory_space=pltpu.VMEM)] * 4,
        out_specs=pl.BlockSpec(memory_space=pltpu.VMEM),
        out_shape=jax.ShapeDtypeStruct((2048, cols), jnp.bfloat16),
        compiler_params=pltpu.CompilerParams(vmem_limit_bytes=VMEM_LIMIT),
        name="order",
    )(tensor.reshape(1).astype(jnp.int32), cotangent, cot_plus, cot_far, cot_minus)

    mask = band_mask(band_index[0], cols)
    new_momentum, kept = None, []
    for c in range(4):
        new_momentum, kept_c = chunk(c, own, others[c], cot, momentum, mask, consts, new_momentum)
        kept.append(kept_c)
    first = over_replicas(jnp.concatenate(kept[:3], 0))
    last = over_replicas(kept[3])
    update = spread(0, first, (rows, cols), backward_consts, None)
    update = spread(6, last, (rows, cols), backward_consts, update)
    return (new_momentum[None], update)


def solution(mesh):
    in_specs = (
        P(("replica", "fsdp", "tensor"), None),
        P(("replica", "fsdp"), "tensor"),
        P("replica", "fsdp", "tensor"),
        P("replica", "fsdp", "tensor", None),
    )
    out_specs = (P("replica", "fsdp", "tensor"), P("fsdp", "tensor"))
    return jax.shard_map(local, mesh=mesh, in_specs=in_specs, out_specs=out_specs, check_vma=False)
```

```python
import functools

import jax
import jax.numpy as jnp
import ml_dtypes
import numpy as np
from jax import lax
from jax.experimental import pallas as pl
from jax.experimental.pallas import tpu as pltpu
from jax.sharding import PartitionSpec as P

SPAN = 64
LOW = 16
TILE = 256
DECAY = 0.999
VMEM_LIMIT = 40 * 1024 * 1024
VMEM = pl.BlockSpec(memory_space=pltpu.VMEM)
HBM = pl.BlockSpec(memory_space=pltpu.HBM)
SMEM = pl.BlockSpec(memory_space=pltpu.SMEM)
PARAMS = pltpu.CompilerParams(vmem_limit_bytes=VMEM_LIMIT)


def split_table(table):
    high = table.astype(ml_dtypes.bfloat16)
    low = (table - high.astype(np.float64)).astype(ml_dtypes.bfloat16)
    return high, low


def tables(cols):
    frequency = np.arange(LOW)[:, None]
    position = np.arange(SPAN)[None, :]
    cosine = np.cos(np.pi * (2.0 * position + 1.0) * frequency / (2.0 * SPAN))
    cosine = cosine * np.where(frequency == 0, np.sqrt(1.0 / SPAN), np.sqrt(2.0 / SPAN))
    down_high, down_low = split_table(np.kron(np.eye(TILE // SPAN), cosine))
    across_high, across_low = split_table(np.kron(np.eye(cols // SPAN), cosine))
    table = np.zeros((640, cols), ml_dtypes.bfloat16)
    table[:128] = across_high
    table[128:256] = across_low
    table[256:320, :TILE], table[320:384, :TILE] = down_high, down_low
    table[384:, :192] = np.concatenate([down_high.T, down_high.T, down_low.T], 1)
    return table


def halves(x):
    high = x.astype(jnp.bfloat16)
    return high, (x - high.astype(jnp.float32)).astype(jnp.bfloat16)


def dot(a, b):
    return jnp.dot(a, b, preferred_element_type=jnp.float32)


def forward(x, table):
    x_high, x_low = halves(x)
    both = dot(table[256:384, :TILE], x_high)
    down_high, down_low = halves(both[:64] + both[64:] + dot(table[256:320, :TILE], x_low))
    turned = (((1,), (1,)), ((), ()))
    stack = jnp.concatenate([down_high, down_low], 0)
    both = lax.dot_general(stack, table[:128, :], turned, preferred_element_type=jnp.float32)
    low = lax.dot_general(down_high, table[128:256, :], turned, preferred_element_type=jnp.float32)
    return both[:64] + both[64:] + low


def backward(coefficients, table):
    high, low = halves(coefficients)
    both = dot(jnp.concatenate([high, low], 0), table[:128, :])
    high, low = halves(both[:64] + both[64:] + dot(high, table[128:256, :]))
    return dot(table[384:, :192], jnp.concatenate([high, low, high], 0))


def order_kernel(place_ref, *refs):
    parts, out_ref = refs[:4], refs[4]
    tensor, sign = place_ref[0], place_ref[1]
    for shift in range(4):
        start = lax.rem(tensor + 4 - sign * shift, 4) * 128
        for d in range(4):
            out_ref[pl.ds((shift * 4 + d) * 128, 128), :] = parts[d][pl.ds(pl.multiple_of(start, 128), 128), :]


def mask_kernel(index_ref, pick_ref, out_ref):
    index = index_ref[...]
    place = index // SPAN * LOW + index % SPAN
    wide = lax.dot_general(
        place.astype(jnp.bfloat16),
        pick_ref[...],
        (((0,), (0,)), ((), ())),
        preferred_element_type=jnp.float32,
    )
    span_rows = index.shape[1]
    lanes = out_ref.shape[1]
    k1 = lax.broadcasted_iota(jnp.int32, (span_rows, LOW, lanes), 1)
    k2 = lax.rem(lax.broadcasted_iota(jnp.int32, (span_rows, LOW, lanes), 2), LOW)
    here = (k1 * LOW + k2).astype(jnp.float32)
    mask = jnp.zeros(here.shape, jnp.float32)
    for j in range(pick_ref.shape[1] // lanes):
        row = wide[:, j * lanes : (j + 1) * lanes]
        mask = jnp.where(row[:, None, :] == here, 1.0, mask)
    out_ref[...] = mask.reshape(out_ref.shape)


def chunk_kernel(*refs):
    own, others = refs[:4], refs[4:8]
    cot_ref, momentum_ref, mask_ref, table = refs[8:12]
    new_ref, kept_ref, lhs = refs[-3:]
    for shift in range(4):
        lhs[pl.ds(shift * 512, 128), :] = own[shift][...]
        lhs[pl.ds(shift * 512 + 128, 384), :] = others[shift][...]
    gradient = lax.dot_general(
        lhs[...], cot_ref[...], (((0,), (0,)), ((), ())), preferred_element_type=jnp.float32
    )
    blended = DECAY * momentum_ref[...] + gradient
    kept = forward(blended, table) * mask_ref[...]
    kept_ref[...] = kept
    new_ref[...] = blended - backward(kept, table)


def chunk(first, steps, own, others, cot, momentum, mask, table, previous, *before):
    rows, cols = momentum.shape
    low_rows, low_cols = TILE // SPAN * LOW, cols // SPAN * LOW
    in_specs = [pl.BlockSpec((128, TILE), lambda i: (0, first + i))] * 4
    in_specs += [pl.BlockSpec((384, TILE), lambda i: (0, i))] * 4
    in_specs += [
        pl.BlockSpec(cot.shape, lambda i: (0, 0)),
        pl.BlockSpec((TILE, cols), lambda i: (first + i, 0)),
        pl.BlockSpec((low_rows, low_cols), lambda i: (first + i, 0)),
        pl.BlockSpec(table.shape, lambda i: (0, 0)),
    ]
    args = [*own, *others, cot, momentum, mask, table, *before]
    aliases = {}
    if previous is not None:
        aliases = {len(args): 0}
        args.append(previous)
    return pl.pallas_call(
        chunk_kernel,
        grid=(steps,),
        in_specs=in_specs + [HBM] * (len(args) - 12),
        out_specs=[
            pl.BlockSpec((TILE, cols), lambda i: (first + i, 0)),
            pl.BlockSpec((low_rows, low_cols), lambda i: (i, 0)),
        ],
        out_shape=[
            jax.ShapeDtypeStruct((rows, cols), jnp.float32),
            jax.ShapeDtypeStruct((steps * low_rows, low_cols), jnp.float32),
        ],
        scratch_shapes=[pltpu.VMEM((2048, TILE), jnp.bfloat16)],
        input_output_aliases=aliases,
        compiler_params=PARAMS,
        cost_estimate=pl.CostEstimate(
            flops=2 * 2048 * TILE * cols * 2 * steps, bytes_accessed=steps * 3 * 2**20, transcendentals=0
        ),
        name=f"chunk{first}",
    )(*args)


def spread_kernel(first, steps, coefficients_ref, table, *refs):
    out_ref, made, sems = refs[-3:]
    low_rows = TILE // SPAN * LOW
    copies = []
    for i in range(steps):
        part = coefficients_ref[pl.ds(i * low_rows, low_rows), :]
        made[i] = backward(part, table).astype(made.dtype)
        rows = pl.ds((first + i) * TILE, TILE)
        copies.append(pltpu.make_async_copy(made.at[i], out_ref.at[rows, :], sems.at[i]))
        copies[-1].start()
    for copy in copies:
        copy.wait()


def spread(coefficients, shape, table):
    rows, cols = shape
    steps = rows // TILE
    return pl.pallas_call(
        lambda *refs: spread_kernel(0, steps, *refs),
        in_specs=[VMEM] * 2,
        out_specs=HBM,
        out_shape=jax.ShapeDtypeStruct(shape, jnp.bfloat16),
        scratch_shapes=[pltpu.VMEM((steps, TILE, cols), jnp.bfloat16), pltpu.SemaphoreType.DMA((steps,))],
        compiler_params=PARAMS,
        cost_estimate=pl.CostEstimate(flops=steps * 10**8, bytes_accessed=steps * 2**18, transcendentals=0),
        name="spread",
    )(coefficients, table)


def pack_kernel(*refs, start, places):
    out, held, loads, stores = refs[-4:]
    rows, width = refs[0].shape[0], out.shape[1]
    coming, going = [], []
    for i in range(places):
        here = held.at[pl.ds(i * rows, rows), :]
        coming.append(pltpu.make_async_copy(refs[i].at[:, pl.ds(start, width)], here, loads.at[i]))
        going.append(pltpu.make_async_copy(here, out.at[pl.ds(i * rows, rows), :], stores.at[i]))
        coming[-1].start()
    for i in range(places):
        coming[i].wait()
        going[i].start()
    for i in range(places):
        going[i].wait()


def pack(parts, start, width, *before):
    places, rows = len(parts), parts[0].shape[0]
    return pl.pallas_call(
        functools.partial(pack_kernel, start=start, places=places),
        in_specs=[HBM] * (places + len(before)),
        out_specs=HBM,
        out_shape=jax.ShapeDtypeStruct((places * rows, width), parts[0].dtype),
        scratch_shapes=[
            pltpu.VMEM((places * rows, width), parts[0].dtype),
            pltpu.SemaphoreType.DMA((places,)),
            pltpu.SemaphoreType.DMA((places,)),
        ],
        compiler_params=PARAMS,
        name="pack",
    )(*parts, *before)


def after(x, *before):
    return pl.pallas_call(
        lambda *refs: None,
        in_specs=[HBM] * (1 + len(before)),
        out_specs=HBM,
        out_shape=jax.ShapeDtypeStruct(x.shape, x.dtype),
        input_output_aliases={0: 0},
        compiler_params=PARAMS,
        name="after",
    )(x, *before)


def apart(x, axis, by):
    pairs = []
    for replica in range(16):
        step = by if replica % 2 == 0 else -by
        pairs += [(replica * 4 + i, replica * 4 + (i + step) % 4) for i in range(4)]
    return lax.ppermute(x, ("replica", axis), pairs)


def around(x, axis, mirrored=False):
    one = apart(x, axis, 1)
    three = apart(x, axis, -1)
    two = apart(three, axis, -1) if mirrored else apart(one, axis, 1)
    return [x, one, two, three]


def swapped(x, partner):
    pairs = []
    for i in range(16):
        z, core = partner(i // 2, i % 2)
        pairs.append((i, z * 2 + core))
    return lax.ppermute(x, "replica", pairs)


def over_replicas(x, core):
    half = x.shape[0] // 2
    mine = lax.dynamic_slice(x, (core * half, 0), (half, x.shape[1]))
    theirs = lax.dynamic_slice(x, ((1 - core) * half, 0), (half, x.shape[1]))
    mine = mine + swapped(theirs, lambda z, c: (z, 1 - c))
    for partner in (lambda z, c: (z ^ 1, c), lambda z, c: (z ^ 2, c), lambda z, c: (7 - z, c)):
        mine = mine + swapped(mine, partner)
    other = swapped(mine, lambda z, c: (z, 1 - c))
    return jnp.where(core == 0, jnp.concatenate([mine, other], 0), jnp.concatenate([other, mine], 0))


def pick_table(span_cols, band):
    pick = np.zeros((span_cols, band, band, span_cols, LOW), np.float32)
    for b in range(span_cols):
        for j in range(band):
            pick[b, j, j, b, :] = 1.0
    return pick.reshape(span_cols * band, band * span_cols * LOW).astype(ml_dtypes.bfloat16)


def local(activations, cotangent, momentum, band_index):
    momentum, band_index = momentum[0], band_index[0]
    rows, cols = momentum.shape
    span_rows, span_cols, band = band_index.shape
    fsdp = lax.axis_index("fsdp")
    tensor = lax.axis_index("tensor")
    core = lax.rem(lax.axis_index("replica"), 2)
    sign = 1 - 2 * core
    table = jnp.asarray(tables(cols))

    def columns(d, start, width):
        owner = lax.rem(fsdp + 4 + sign * d, 4)
        return lax.dynamic_slice(activations, (0, owner * rows + start), (activations.shape[0], width))

    mine = columns(0, 0, rows)
    own = around(mine, "tensor")
    pieces = [columns(d, 0, 512) for d in (1, 2, 3)] + [columns(d, 512, 1536) for d in (1, 2, 3)]
    early = [apart(pieces[d - 1], "fsdp", d) for d in (1, 2, 3)]
    late_one = apart(after(pieces[3], own[1], *early), "fsdp", 1)
    late_three = apart(after(pieces[5], own[1], *early), "fsdp", 3)
    late = [late_one, apart(after(pieces[4], late_one), "fsdp", 2), late_three]
    cots = around(pack([cotangent], 0, cols, late_one, late_three), "fsdp")

    chunks = [(0, 2), (2, 3), (5, 2), (7, 1)]
    units = [own]
    for first, steps in chunks:
        if first == 0:
            unit = pack(early, 0, 512, own[1], own[3])
        else:
            before = {2: [own[2], units[-1][1], units[-1][3]], 5: [units[-2][2], units[-1][1]], 7: []}[first]
            unit = pack(late, first * TILE - 512, steps * TILE, *before)
        units.append(around(unit, "tensor", first in (0, 2, 7)))
    others = units[1:]

    cot = pl.pallas_call(
        order_kernel,
        in_specs=[SMEM] + [VMEM] * 4,
        out_specs=VMEM,
        out_shape=jax.ShapeDtypeStruct((2048, cols), jnp.bfloat16),
        compiler_params=PARAMS,
        name="order",
    )(jnp.stack([tensor, sign]).astype(jnp.int32), *cots)

    mask = pl.pallas_call(
        mask_kernel,
        in_specs=[VMEM] * 2,
        out_specs=VMEM,
        out_shape=jax.ShapeDtypeStruct((span_rows * LOW, span_cols * LOW), jnp.float32),
        compiler_params=PARAMS,
        name="mask",
    )(band_index.transpose(1, 2, 0).reshape(span_cols * band, span_rows), jnp.asarray(pick_table(span_cols, band)))

    def part(i, previous, *before):
        first, steps = chunks[i]
        return chunk(first, steps, own, others[i], cot, momentum, mask, table, previous, *before)

    new_momentum, kept = None, []
    for i in range(len(chunks)):
        new_momentum, kept_i = part(i, new_momentum)
        kept.append(kept_i)
    combined = over_replicas(jnp.concatenate(kept, 0), core)
    update = spread(combined, (rows, cols), table)
    return (new_momentum[None], update)


def solution(mesh):
    in_specs = (
        P(("replica", "fsdp", "tensor"), None),
        P(("replica", "fsdp"), "tensor"),
        P("replica", "fsdp", "tensor"),
        P("replica", "fsdp", "tensor", None),
    )
    out_specs = (P("replica", "fsdp", "tensor"), P("fsdp", "tensor"))
    return jax.shard_map(local, mesh=mesh, in_specs=in_specs, out_specs=out_specs, check_vma=False)
```

```python
import functools

import jax
import jax.numpy as jnp
import ml_dtypes
import numpy as np
from jax import lax
from jax.experimental import pallas as pl
from jax.experimental.pallas import tpu as pltpu
from jax.sharding import PartitionSpec as P

SPAN = 64
LOW = 16
TILE = 256
DECAY = 0.999
VMEM_LIMIT = 40 * 1024 * 1024
VMEM = pl.BlockSpec(memory_space=pltpu.VMEM)
HBM = pl.BlockSpec(memory_space=pltpu.HBM)
SMEM = pl.BlockSpec(memory_space=pltpu.SMEM)
PARAMS = pltpu.CompilerParams(vmem_limit_bytes=VMEM_LIMIT)


def split_table(table):
    high = table.astype(ml_dtypes.bfloat16)
    low = (table - high.astype(np.float64)).astype(ml_dtypes.bfloat16)
    return high, low


def tables(cols):
    frequency = np.arange(LOW)[:, None]
    position = np.arange(SPAN)[None, :]
    cosine = np.cos(np.pi * (2.0 * position + 1.0) * frequency / (2.0 * SPAN))
    cosine = cosine * np.where(frequency == 0, np.sqrt(1.0 / SPAN), np.sqrt(2.0 / SPAN))
    down_high, down_low = split_table(np.kron(np.eye(TILE // SPAN), cosine))
    across_high, across_low = split_table(np.kron(np.eye(cols // SPAN), cosine))
    table = np.zeros((640, cols), ml_dtypes.bfloat16)
    table[:128] = across_high
    table[128:256] = across_low
    table[256:320, :TILE], table[320:384, :TILE] = down_high, down_low
    table[384:, :192] = np.concatenate([down_high.T, down_high.T, down_low.T], 1)
    return table


def halves(x):
    high = x.astype(jnp.bfloat16)
    return high, (x - high.astype(jnp.float32)).astype(jnp.bfloat16)


def dot(a, b):
    return jnp.dot(a, b, preferred_element_type=jnp.float32)


def forward(x, table):
    x_high, x_low = halves(x)
    both = dot(table[256:384, :TILE], x_high)
    down_high, down_low = halves(both[:64] + both[64:] + dot(table[256:320, :TILE], x_low))
    turned = (((1,), (1,)), ((), ()))
    stack = jnp.concatenate([down_high, down_low], 0)
    both = lax.dot_general(stack, table[:128, :], turned, preferred_element_type=jnp.float32)
    low = lax.dot_general(down_high, table[128:256, :], turned, preferred_element_type=jnp.float32)
    return both[:64] + both[64:] + low


def backward(coefficients, table):
    high, low = halves(coefficients)
    both = dot(jnp.concatenate([high, low], 0), table[:128, :])
    high, low = halves(both[:64] + both[64:] + dot(high, table[128:256, :]))
    return dot(table[384:, :192], jnp.concatenate([high, low, high], 0))


def order_kernel(place_ref, *refs):
    parts, out_ref = refs[:4], refs[4]
    tensor, sign = place_ref[0], place_ref[1]
    for shift in range(4):
        start = lax.rem(tensor + 4 - sign * shift, 4) * 128
        for d in range(4):
            out_ref[pl.ds((shift * 4 + d) * 128, 128), :] = parts[d][pl.ds(pl.multiple_of(start, 128), 128), :]


def mask_kernel(index_ref, pick_ref, out_ref):
    index = index_ref[...]
    place = index // SPAN * LOW + index % SPAN
    wide = lax.dot_general(
        place.astype(jnp.bfloat16),
        pick_ref[...],
        (((0,), (0,)), ((), ())),
        preferred_element_type=jnp.float32,
    )
    span_rows = index.shape[1]
    lanes = out_ref.shape[1]
    k1 = lax.broadcasted_iota(jnp.int32, (span_rows, LOW, lanes), 1)
    k2 = lax.rem(lax.broadcasted_iota(jnp.int32, (span_rows, LOW, lanes), 2), LOW)
    here = (k1 * LOW + k2).astype(jnp.float32)
    mask = jnp.zeros(here.shape, jnp.float32)
    for j in range(pick_ref.shape[1] // lanes):
        row = wide[:, j * lanes : (j + 1) * lanes]
        mask = jnp.where(row[:, None, :] == here, 1.0, mask)
    out_ref[...] = mask.reshape(out_ref.shape)


def chunk_kernel(*refs):
    own, others = refs[:4], refs[4:8]
    cot_ref, momentum_ref, mask_ref, table = refs[8:12]
    new_ref, kept_ref, lhs = refs[-3:]
    for shift in range(4):
        lhs[pl.ds(shift * 512, 128), :] = own[shift][...]
        lhs[pl.ds(shift * 512 + 128, 384), :] = others[shift][...]
    gradient = lax.dot_general(
        lhs[...], cot_ref[...], (((0,), (0,)), ((), ())), preferred_element_type=jnp.float32
    )
    blended = DECAY * momentum_ref[...] + gradient
    kept = forward(blended, table) * mask_ref[...]
    kept_ref[...] = kept
    new_ref[...] = blended - backward(kept, table)


def chunk(first, steps, own, others, cot, momentum, mask, table, previous, *before):
    rows, cols = momentum.shape
    low_rows, low_cols = TILE // SPAN * LOW, cols // SPAN * LOW
    in_specs = [pl.BlockSpec((128, TILE), lambda i: (0, first + i))] * 4
    in_specs += [pl.BlockSpec((384, TILE), lambda i: (0, i))] * 4
    in_specs += [
        pl.BlockSpec(cot.shape, lambda i: (0, 0)),
        pl.BlockSpec((TILE, cols), lambda i: (first + i, 0)),
        pl.BlockSpec((low_rows, low_cols), lambda i: (first + i, 0)),
        pl.BlockSpec(table.shape, lambda i: (0, 0)),
    ]
    args = [*own, *others, cot, momentum, mask, table, *before]
    aliases = {}
    if previous is not None:
        aliases = {len(args): 0}
        args.append(previous)
    return pl.pallas_call(
        chunk_kernel,
        grid=(steps,),
        in_specs=in_specs + [HBM] * (len(args) - 12),
        out_specs=[
            pl.BlockSpec((TILE, cols), lambda i: (first + i, 0)),
            pl.BlockSpec((low_rows, low_cols), lambda i: (i, 0)),
        ],
        out_shape=[
            jax.ShapeDtypeStruct((rows, cols), jnp.float32),
            jax.ShapeDtypeStruct((steps * low_rows, low_cols), jnp.float32),
        ],
        scratch_shapes=[pltpu.VMEM((2048, TILE), jnp.bfloat16)],
        input_output_aliases=aliases,
        compiler_params=PARAMS,
        cost_estimate=pl.CostEstimate(
            flops=2 * 2048 * TILE * cols * 2 * steps, bytes_accessed=steps * 3 * 2**20, transcendentals=0
        ),
        name=f"chunk{first}",
    )(*args)


def spread_kernel(first, steps, coefficients_ref, table, *refs):
    out_ref, made, sems = refs[-3:]
    low_rows = TILE // SPAN * LOW
    copies = []
    for i in range(steps):
        part = coefficients_ref[pl.ds(i * low_rows, low_rows), :]
        made[i] = backward(part, table).astype(made.dtype)
        rows = pl.ds((first + i) * TILE, TILE)
        copies.append(pltpu.make_async_copy(made.at[i], out_ref.at[rows, :], sems.at[i]))
        copies[-1].start()
    for copy in copies:
        copy.wait()


def spread(coefficients, shape, table):
    rows, cols = shape
    steps = rows // TILE
    return pl.pallas_call(
        lambda *refs: spread_kernel(0, steps, *refs),
        in_specs=[VMEM] * 2,
        out_specs=HBM,
        out_shape=jax.ShapeDtypeStruct(shape, jnp.bfloat16),
        scratch_shapes=[pltpu.VMEM((steps, TILE, cols), jnp.bfloat16), pltpu.SemaphoreType.DMA((steps,))],
        compiler_params=PARAMS,
        cost_estimate=pl.CostEstimate(flops=steps * 10**8, bytes_accessed=steps * 2**18, transcendentals=0),
        name="spread",
    )(coefficients, table)


def pack_kernel(*refs, start, places):
    out, held, loads, stores = refs[-4:]
    rows, width = refs[0].shape[0], out.shape[1]
    coming, going = [], []
    for i in range(places):
        here = held.at[pl.ds(i * rows, rows), :]
        coming.append(pltpu.make_async_copy(refs[i].at[:, pl.ds(start, width)], here, loads.at[i]))
        going.append(pltpu.make_async_copy(here, out.at[pl.ds(i * rows, rows), :], stores.at[i]))
        coming[-1].start()
    for i in range(places):
        coming[i].wait()
        going[i].start()
    for i in range(places):
        going[i].wait()


def pack(parts, start, width, *before):
    places, rows = len(parts), parts[0].shape[0]
    return pl.pallas_call(
        functools.partial(pack_kernel, start=start, places=places),
        in_specs=[HBM] * (places + len(before)),
        out_specs=HBM,
        out_shape=jax.ShapeDtypeStruct((places * rows, width), parts[0].dtype),
        scratch_shapes=[
            pltpu.VMEM((places * rows, width), parts[0].dtype),
            pltpu.SemaphoreType.DMA((places,)),
            pltpu.SemaphoreType.DMA((places,)),
        ],
        compiler_params=PARAMS,
        name="pack",
    )(*parts, *before)


def after(x, *before):
    return pl.pallas_call(
        lambda *refs: None,
        in_specs=[HBM] * (1 + len(before)),
        out_specs=HBM,
        out_shape=jax.ShapeDtypeStruct(x.shape, x.dtype),
        input_output_aliases={0: 0},
        compiler_params=PARAMS,
        name="after",
    )(x, *before)


def apart(x, axis, by):
    pairs = []
    for replica in range(16):
        step = by if replica % 2 == 0 else -by
        pairs += [(replica * 4 + i, replica * 4 + (i + step) % 4) for i in range(4)]
    return lax.ppermute(x, ("replica", axis), pairs)


def around(x, axis, mirrored=False):
    one = apart(x, axis, 1)
    three = apart(x, axis, -1)
    two = apart(three, axis, -1) if mirrored else apart(one, axis, 1)
    return [x, one, two, three]


def swapped(x, partner):
    pairs = []
    for i in range(16):
        z, core = partner(i // 2, i % 2)
        pairs.append((i, z * 2 + core))
    return lax.ppermute(x, "replica", pairs)


def over_replicas(x, core):
    half = x.shape[0] // 2
    mine = lax.dynamic_slice(x, (core * half, 0), (half, x.shape[1]))
    theirs = lax.dynamic_slice(x, ((1 - core) * half, 0), (half, x.shape[1]))
    mine = mine + swapped(theirs, lambda z, c: (z, 1 - c))
    def quad(z, c):
        return (((z - 2 * c) % 8 ^ 2) + 2 * c) % 8, c

    for partner in (lambda z, c: (z ^ 1, c), quad, lambda z, c: ((7 + 4 * c - z) % 8, c)):
        mine = mine + swapped(mine, partner)
    other = swapped(mine, lambda z, c: (z, 1 - c))
    return jnp.where(core == 0, jnp.concatenate([mine, other], 0), jnp.concatenate([other, mine], 0))


def pick_table(span_cols, band):
    pick = np.zeros((span_cols, band, band, span_cols, LOW), np.float32)
    for b in range(span_cols):
        for j in range(band):
            pick[b, j, j, b, :] = 1.0
    return pick.reshape(span_cols * band, band * span_cols * LOW).astype(ml_dtypes.bfloat16)


def local(activations, cotangent, momentum, band_index):
    momentum, band_index = momentum[0], band_index[0]
    rows, cols = momentum.shape
    span_rows, span_cols, band = band_index.shape
    fsdp = lax.axis_index("fsdp")
    tensor = lax.axis_index("tensor")
    core = lax.rem(lax.axis_index("replica"), 2)
    sign = 1 - 2 * core
    table = jnp.asarray(tables(cols))

    def columns(d, start, width):
        owner = lax.rem(fsdp + 4 + sign * d, 4)
        return lax.dynamic_slice(activations, (0, owner * rows + start), (activations.shape[0], width))

    mine = columns(0, 0, rows)
    own = around(mine, "tensor")
    pieces = [columns(d, 0, 768) for d in (1, 2, 3)] + [columns(d, 768, 1280) for d in (1, 2, 3)]
    early = [apart(pieces[d - 1], "fsdp", d) for d in (1, 2, 3)]
    late_one = apart(after(pieces[3], own[1], *early), "fsdp", 1)
    late_three = apart(after(pieces[5], own[1], *early), "fsdp", 3)
    late = [late_one, apart(after(pieces[4], late_one), "fsdp", 2), late_three]
    cots = around(pack([cotangent], 0, cols, late_one), "fsdp")

    chunks = [(0, 3), (3, 2), (5, 3)]
    units = [own]
    for first, steps in chunks:
        if first == 0:
            unit = pack(early, 0, 768, own[1], own[3])
        else:
            before = [units[-1][1], units[-1][3]] if first == 3 else [own[2], units[-2][2], units[-1][1]]
            unit = pack(late, first * TILE - 768, steps * TILE, *before)
        units.append(around(unit, "tensor", first in (0, 5)))
    others = units[1:]

    cot = pl.pallas_call(
        order_kernel,
        in_specs=[SMEM] + [VMEM] * 4,
        out_specs=VMEM,
        out_shape=jax.ShapeDtypeStruct((2048, cols), jnp.bfloat16),
        compiler_params=PARAMS,
        name="order",
    )(jnp.stack([tensor, sign]).astype(jnp.int32), *cots)

    mask = pl.pallas_call(
        mask_kernel,
        in_specs=[VMEM] * 2,
        out_specs=VMEM,
        out_shape=jax.ShapeDtypeStruct((span_rows * LOW, span_cols * LOW), jnp.float32),
        compiler_params=PARAMS,
        name="mask",
    )(band_index.transpose(1, 2, 0).reshape(span_cols * band, span_rows), jnp.asarray(pick_table(span_cols, band)))

    def part(i, previous, *before):
        first, steps = chunks[i]
        return chunk(first, steps, own, others[i], cot, momentum, mask, table, previous, *before)

    new_momentum, kept = None, []
    for i in range(len(chunks)):
        new_momentum, kept_i = part(i, new_momentum)
        kept.append(kept_i)
    combined = over_replicas(jnp.concatenate(kept, 0), core)
    update = spread(combined, (rows, cols), table)
    return (new_momentum[None], update)


def solution(mesh):
    in_specs = (
        P(("replica", "fsdp", "tensor"), None),
        P(("replica", "fsdp"), "tensor"),
        P("replica", "fsdp", "tensor"),
        P("replica", "fsdp", "tensor", None),
    )
    out_specs = (P("replica", "fsdp", "tensor"), P("fsdp", "tensor"))
    return jax.shard_map(local, mesh=mesh, in_specs=in_specs, out_specs=out_specs, check_vma=False)
```

```python
import functools

import jax
import jax.numpy as jnp
import ml_dtypes
import numpy as np
from jax import lax
from jax.experimental import pallas as pl
from jax.experimental.pallas import tpu as pltpu
from jax.sharding import PartitionSpec as P

SPAN = 64
LOW = 16
TILE = 256
DECAY = 0.999
VMEM_LIMIT = 40 * 1024 * 1024
VMEM = pl.BlockSpec(memory_space=pltpu.VMEM)
HBM = pl.BlockSpec(memory_space=pltpu.HBM)
SMEM = pl.BlockSpec(memory_space=pltpu.SMEM)
PARAMS = pltpu.CompilerParams(vmem_limit_bytes=VMEM_LIMIT)


def split_table(table):
    high = table.astype(ml_dtypes.bfloat16)
    low = (table - high.astype(np.float64)).astype(ml_dtypes.bfloat16)
    return high, low


def tables(cols):
    frequency = np.arange(LOW)[:, None]
    position = np.arange(SPAN)[None, :]
    cosine = np.cos(np.pi * (2.0 * position + 1.0) * frequency / (2.0 * SPAN))
    cosine = cosine * np.where(frequency == 0, np.sqrt(1.0 / SPAN), np.sqrt(2.0 / SPAN))
    down_high, down_low = split_table(np.kron(np.eye(TILE // SPAN), cosine))
    across_high, across_low = split_table(np.kron(np.eye(cols // SPAN), cosine))
    table = np.zeros((640, cols), ml_dtypes.bfloat16)
    table[:128] = across_high
    table[128:256] = across_low
    table[256:320, :TILE], table[320:384, :TILE] = down_high, down_low
    table[384:, :192] = np.concatenate([down_high.T, down_high.T, down_low.T], 1)
    return table


def halves(x):
    high = x.astype(jnp.bfloat16)
    return high, (x - high.astype(jnp.float32)).astype(jnp.bfloat16)


def dot(a, b):
    return jnp.dot(a, b, preferred_element_type=jnp.float32)


def forward(x, table):
    x_high, x_low = halves(x)
    both = dot(table[256:384, :TILE], x_high)
    down_high, down_low = halves(both[:64] + both[64:] + dot(table[256:320, :TILE], x_low))
    turned = (((1,), (1,)), ((), ()))
    stack = jnp.concatenate([down_high, down_low], 0)
    both = lax.dot_general(stack, table[:128, :], turned, preferred_element_type=jnp.float32)
    low = lax.dot_general(down_high, table[128:256, :], turned, preferred_element_type=jnp.float32)
    return both[:64] + both[64:] + low


def backward(coefficients, table):
    high, low = halves(coefficients)
    both = dot(jnp.concatenate([high, low], 0), table[:128, :])
    high, low = halves(both[:64] + both[64:] + dot(high, table[128:256, :]))
    return dot(table[384:, :192], jnp.concatenate([high, low, high], 0))


def order_kernel(place_ref, *refs):
    parts, out_ref = refs[:4], refs[4]
    tensor, sign = place_ref[0], place_ref[1]
    for shift in range(4):
        start = lax.rem(tensor + 4 - sign * shift, 4) * 128
        for d in range(4):
            out_ref[pl.ds((shift * 4 + d) * 128, 128), :] = parts[d][pl.ds(pl.multiple_of(start, 128), 128), :]


def mask_kernel(index_ref, pick_ref, out_ref):
    index = index_ref[...]
    place = index // SPAN * LOW + index % SPAN
    wide = lax.dot_general(
        place.astype(jnp.bfloat16),
        pick_ref[...],
        (((0,), (0,)), ((), ())),
        preferred_element_type=jnp.float32,
    )
    span_rows = index.shape[1]
    lanes = out_ref.shape[1]
    k1 = lax.broadcasted_iota(jnp.int32, (span_rows, LOW, lanes), 1)
    k2 = lax.rem(lax.broadcasted_iota(jnp.int32, (span_rows, LOW, lanes), 2), LOW)
    here = (k1 * LOW + k2).astype(jnp.float32)
    mask = jnp.zeros(here.shape, jnp.float32)
    for j in range(pick_ref.shape[1] // lanes):
        row = wide[:, j * lanes : (j + 1) * lanes]
        mask = jnp.where(row[:, None, :] == here, 1.0, mask)
    out_ref[...] = mask.reshape(out_ref.shape)


def chunk_kernel(*refs):
    own, others = refs[:4], refs[4:8]
    cot_ref, momentum_ref, mask_ref, table = refs[8:12]
    new_ref, kept_ref, lhs = refs[-3:]
    for shift in range(4):
        lhs[pl.ds(shift * 512, 128), :] = own[shift][...]
        lhs[pl.ds(shift * 512 + 128, 384), :] = others[shift][...]
    gradient = lax.dot_general(
        lhs[...], cot_ref[...], (((0,), (0,)), ((), ())), preferred_element_type=jnp.float32
    )
    blended = DECAY * momentum_ref[...] + gradient
    kept = forward(blended, table) * mask_ref[...]
    kept_ref[...] = kept
    new_ref[...] = blended - backward(kept, table)


def chunk(first, steps, own, others, cot, momentum, mask, table, previous, *before):
    rows, cols = momentum.shape
    low_rows, low_cols = TILE // SPAN * LOW, cols // SPAN * LOW
    in_specs = [pl.BlockSpec((128, TILE), lambda i: (0, first + i))] * 4
    in_specs += [pl.BlockSpec((384, TILE), lambda i: (0, i))] * 4
    in_specs += [
        pl.BlockSpec(cot.shape, lambda i: (0, 0)),
        pl.BlockSpec((TILE, cols), lambda i: (first + i, 0)),
        pl.BlockSpec((low_rows, low_cols), lambda i: (first + i, 0)),
        pl.BlockSpec(table.shape, lambda i: (0, 0)),
    ]
    args = [*own, *others, cot, momentum, mask, table, *before]
    aliases = {}
    if previous is not None:
        aliases = {len(args): 0}
        args.append(previous)
    return pl.pallas_call(
        chunk_kernel,
        grid=(steps,),
        in_specs=in_specs + [HBM] * (len(args) - 12),
        out_specs=[
            pl.BlockSpec((TILE, cols), lambda i: (first + i, 0)),
            pl.BlockSpec((low_rows, low_cols), lambda i: (i, 0)),
        ],
        out_shape=[
            jax.ShapeDtypeStruct((rows, cols), jnp.float32),
            jax.ShapeDtypeStruct((steps * low_rows, low_cols), jnp.float32),
        ],
        scratch_shapes=[pltpu.VMEM((2048, TILE), jnp.bfloat16)],
        input_output_aliases=aliases,
        compiler_params=PARAMS,
        cost_estimate=pl.CostEstimate(
            flops=2 * 2048 * TILE * cols * 2 * steps, bytes_accessed=steps * 3 * 2**20, transcendentals=0
        ),
        name=f"chunk{first}",
    )(*args)


def spread_kernel(first, steps, coefficients_ref, table, *refs):
    out_ref, made, sems = refs[-3:]
    low_rows = TILE // SPAN * LOW
    copies = []
    for i in range(steps):
        part = coefficients_ref[pl.ds(i * low_rows, low_rows), :]
        made[i] = backward(part, table).astype(made.dtype)
        rows = pl.ds((first + i) * TILE, TILE)
        copies.append(pltpu.make_async_copy(made.at[i], out_ref.at[rows, :], sems.at[i]))
        copies[-1].start()
    for copy in copies:
        copy.wait()


def spread(coefficients, shape, table):
    rows, cols = shape
    steps = rows // TILE
    return pl.pallas_call(
        lambda *refs: spread_kernel(0, steps, *refs),
        in_specs=[VMEM] * 2,
        out_specs=HBM,
        out_shape=jax.ShapeDtypeStruct(shape, jnp.bfloat16),
        scratch_shapes=[pltpu.VMEM((steps, TILE, cols), jnp.bfloat16), pltpu.SemaphoreType.DMA((steps,))],
        compiler_params=PARAMS,
        cost_estimate=pl.CostEstimate(flops=steps * 10**8, bytes_accessed=steps * 2**18, transcendentals=0),
        name="spread",
    )(coefficients, table)


def pack_kernel(*refs, start, places):
    out, held, loads, stores = refs[-4:]
    rows, width = refs[0].shape[0], out.shape[1]
    coming, going = [], []
    for i in range(places):
        here = held.at[pl.ds(i * rows, rows), :]
        coming.append(pltpu.make_async_copy(refs[i].at[:, pl.ds(start, width)], here, loads.at[i]))
        going.append(pltpu.make_async_copy(here, out.at[pl.ds(i * rows, rows), :], stores.at[i]))
        coming[-1].start()
    for i in range(places):
        coming[i].wait()
        going[i].start()
    for i in range(places):
        going[i].wait()


def pack(parts, start, width, *before):
    places, rows = len(parts), parts[0].shape[0]
    return pl.pallas_call(
        functools.partial(pack_kernel, start=start, places=places),
        in_specs=[HBM] * (places + len(before)),
        out_specs=HBM,
        out_shape=jax.ShapeDtypeStruct((places * rows, width), parts[0].dtype),
        scratch_shapes=[
            pltpu.VMEM((places * rows, width), parts[0].dtype),
            pltpu.SemaphoreType.DMA((places,)),
            pltpu.SemaphoreType.DMA((places,)),
        ],
        compiler_params=PARAMS,
        name="pack",
    )(*parts, *before)


def after(x, *before):
    return pl.pallas_call(
        lambda *refs: None,
        in_specs=[HBM] * (1 + len(before)),
        out_specs=HBM,
        out_shape=jax.ShapeDtypeStruct(x.shape, x.dtype),
        input_output_aliases={0: 0},
        compiler_params=PARAMS,
        name="after",
    )(x, *before)


def apart(x, axis, by):
    pairs = []
    for replica in range(16):
        step = by if replica % 2 == 0 else -by
        pairs += [(replica * 4 + i, replica * 4 + (i + step) % 4) for i in range(4)]
    return lax.ppermute(x, ("replica", axis), pairs)


def around(x, axis, mirrored=False):
    one = apart(x, axis, 1)
    three = apart(x, axis, -1)
    two = apart(three, axis, -1) if mirrored else apart(one, axis, 1)
    return [x, one, two, three]


def swapped(x, partner):
    pairs = []
    for i in range(16):
        z, core = partner(i // 2, i % 2)
        pairs.append((i, z * 2 + core))
    return lax.ppermute(x, "replica", pairs)


def halve_kernel(core_ref, *refs):
    parts, mine, theirs = refs[:-2], refs[-2], refs[-1]
    half, start = mine.shape[0], 0
    for part in parts:
        for row in range(0, part.shape[0], 64):
            upper = (start + row) // half
            value = part[pl.ds(row, 64), :]
            here = pl.ds((start + row) % half, 64)

            @pl.when(core_ref[0] == upper)
            def _():
                mine[here, :] = value

            @pl.when(core_ref[0] != upper)
            def _():
                theirs[here, :] = value

        start += part.shape[0]


def over_replicas(parts, core):
    half = jax.ShapeDtypeStruct((sum(p.shape[0] for p in parts) // 2, parts[0].shape[1]), parts[0].dtype)
    mine, theirs = pl.pallas_call(
        halve_kernel,
        in_specs=[SMEM] + [VMEM] * len(parts),
        out_specs=[VMEM] * 2,
        out_shape=[half, half],
        compiler_params=PARAMS,
        name="halve",
    )(core.reshape(1).astype(jnp.int32), *parts)
    mine = mine + swapped(theirs, lambda z, c: (z, 1 - c))
    def quad(z, c):
        return (((z - 2 * c) % 8 ^ 2) + 2 * c) % 8, c

    for partner in (lambda z, c: (z ^ 1, c), quad, lambda z, c: ((7 + 4 * c - z) % 8, c)):
        mine = mine + swapped(mine, partner)
    other = swapped(mine, lambda z, c: (z, 1 - c))
    return jnp.where(core == 0, jnp.concatenate([mine, other], 0), jnp.concatenate([other, mine], 0))


def pick_table(span_cols, band):
    pick = np.zeros((span_cols, band, band, span_cols, LOW), np.float32)
    for b in range(span_cols):
        for j in range(band):
            pick[b, j, j, b, :] = 1.0
    return pick.reshape(span_cols * band, band * span_cols * LOW).astype(ml_dtypes.bfloat16)


def local(activations, cotangent, momentum, band_index):
    momentum, band_index = momentum[0], band_index[0]
    rows, cols = momentum.shape
    span_rows, span_cols, band = band_index.shape
    fsdp = lax.axis_index("fsdp")
    tensor = lax.axis_index("tensor")
    core = lax.rem(lax.axis_index("replica"), 2)
    sign = 1 - 2 * core
    table = jnp.asarray(tables(cols))

    def columns(d, start, width):
        owner = lax.rem(fsdp + 4 + sign * d, 4)
        return lax.dynamic_slice(activations, (0, owner * rows + start), (activations.shape[0], width))

    mine = columns(0, 0, rows)
    own = around(mine, "tensor")
    pieces = [columns(d, 0, 768) for d in (1, 2, 3)] + [columns(d, 768, 1280) for d in (1, 2, 3)]
    early = [apart(pieces[d - 1], "fsdp", d) for d in (1, 2, 3)]
    late_one = apart(after(pieces[3], own[1], *early), "fsdp", 1)
    late_three = apart(after(pieces[5], own[1], *early), "fsdp", 3)
    late = [late_one, apart(after(pieces[4], late_one), "fsdp", 2), late_three]
    cots = around(pack([cotangent], 0, cols, late_one), "fsdp")

    chunks = [(0, 3), (3, 4), (7, 1)]
    units = [own]
    for first, steps in chunks:
        if first == 0:
            unit = pack(early, 0, 768, own[1], own[3])
        else:
            before = [units[-1][1], units[-1][3]] if first == 3 else [own[2], units[-2][2], units[-1][1]]
            unit = pack(late, first * TILE - 768, steps * TILE, *before)
        units.append(around(unit, "tensor", first in (0, 7)))
    others = units[1:]

    cot = pl.pallas_call(
        order_kernel,
        in_specs=[SMEM] + [VMEM] * 4,
        out_specs=VMEM,
        out_shape=jax.ShapeDtypeStruct((2048, cols), jnp.bfloat16),
        compiler_params=PARAMS,
        name="order",
    )(jnp.stack([tensor, sign]).astype(jnp.int32), *cots)

    mask = pl.pallas_call(
        mask_kernel,
        in_specs=[VMEM] * 2,
        out_specs=VMEM,
        out_shape=jax.ShapeDtypeStruct((span_rows * LOW, span_cols * LOW), jnp.float32),
        compiler_params=PARAMS,
        name="mask",
    )(band_index.transpose(1, 2, 0).reshape(span_cols * band, span_rows), jnp.asarray(pick_table(span_cols, band)))

    def part(i, previous, *before):
        first, steps = chunks[i]
        return chunk(first, steps, own, others[i], cot, momentum, mask, table, previous, *before)

    new_momentum, kept = None, []
    for i in range(len(chunks)):
        new_momentum, kept_i = part(i, new_momentum)
        kept.append(kept_i)
    combined = over_replicas(kept, core)
    update = spread(combined, (rows, cols), table)
    return (new_momentum[None], update)


def solution(mesh):
    in_specs = (
        P(("replica", "fsdp", "tensor"), None),
        P(("replica", "fsdp"), "tensor"),
        P("replica", "fsdp", "tensor"),
        P("replica", "fsdp", "tensor", None),
    )
    out_specs = (P("replica", "fsdp", "tensor"), P("fsdp", "tensor"))
    return jax.shard_map(local, mesh=mesh, in_specs=in_specs, out_specs=out_specs, check_vma=False)
```

```python
import functools

import jax
import jax.numpy as jnp
import ml_dtypes
import numpy as np
from jax import lax
from jax.experimental import pallas as pl
from jax.experimental.pallas import tpu as pltpu
from jax.sharding import PartitionSpec as P

SPAN = 64
LOW = 16
TILE = 256
DECAY = 0.999
VMEM_LIMIT = 40 * 1024 * 1024
VMEM = pl.BlockSpec(memory_space=pltpu.VMEM)
HBM = pl.BlockSpec(memory_space=pltpu.HBM)
SMEM = pl.BlockSpec(memory_space=pltpu.SMEM)
PARAMS = pltpu.CompilerParams(vmem_limit_bytes=VMEM_LIMIT)


def split_table(table):
    high = table.astype(ml_dtypes.bfloat16)
    low = (table - high.astype(np.float64)).astype(ml_dtypes.bfloat16)
    return high, low


def tables(cols):
    frequency = np.arange(LOW)[:, None]
    position = np.arange(SPAN)[None, :]
    cosine = np.cos(np.pi * (2.0 * position + 1.0) * frequency / (2.0 * SPAN))
    cosine = cosine * np.where(frequency == 0, np.sqrt(1.0 / SPAN), np.sqrt(2.0 / SPAN))
    down_high, down_low = split_table(np.kron(np.eye(TILE // SPAN), cosine))
    across_high, across_low = split_table(np.kron(np.eye(cols // SPAN), cosine))
    table = np.zeros((640, cols), ml_dtypes.bfloat16)
    table[:128] = across_high
    table[128:256] = across_low
    table[256:320, :TILE], table[320:384, :TILE] = down_high, down_low
    table[384:, :192] = np.concatenate([down_high.T, down_high.T, down_low.T], 1)
    return table


def halves(x):
    high = x.astype(jnp.bfloat16)
    return high, (x - high.astype(jnp.float32)).astype(jnp.bfloat16)


def dot(a, b):
    return jnp.dot(a, b, preferred_element_type=jnp.float32)


def forward(x, table):
    x_high, x_low = halves(x)
    both = dot(table[256:384, :TILE], x_high)
    down_high, down_low = halves(both[:64] + both[64:] + dot(table[256:320, :TILE], x_low))
    turned = (((1,), (1,)), ((), ()))
    stack = jnp.concatenate([down_high, down_low], 0)
    both = lax.dot_general(stack, table[:128, :], turned, preferred_element_type=jnp.float32)
    low = lax.dot_general(down_high, table[128:256, :], turned, preferred_element_type=jnp.float32)
    return both[:64] + both[64:] + low


def backward(coefficients, table):
    high, low = halves(coefficients)
    both = dot(jnp.concatenate([high, low], 0), table[:128, :])
    high, low = halves(both[:64] + both[64:] + dot(high, table[128:256, :]))
    return dot(table[384:, :192], jnp.concatenate([high, low, high], 0))


def order_kernel(place_ref, *refs):
    parts, out_ref = refs[:4], refs[4]
    tensor, sign = place_ref[0], place_ref[1]
    for shift in range(4):
        start = lax.rem(tensor + 4 - sign * shift, 4) * 128
        for d in range(4):
            out_ref[pl.ds((shift * 4 + d) * 128, 128), :] = parts[d][pl.ds(pl.multiple_of(start, 128), 128), :]


def mask_kernel(index_ref, pick_ref, out_ref):
    index = index_ref[...]
    place = index // SPAN * LOW + index % SPAN
    wide = lax.dot_general(
        place.astype(jnp.bfloat16),
        pick_ref[...],
        (((0,), (0,)), ((), ())),
        preferred_element_type=jnp.float32,
    )
    span_rows = index.shape[1]
    lanes = out_ref.shape[1]
    k1 = lax.broadcasted_iota(jnp.int32, (span_rows, LOW, lanes), 1)
    k2 = lax.rem(lax.broadcasted_iota(jnp.int32, (span_rows, LOW, lanes), 2), LOW)
    here = (k1 * LOW + k2).astype(jnp.float32)
    mask = jnp.zeros(here.shape, jnp.float32)
    for j in range(pick_ref.shape[1] // lanes):
        row = wide[:, j * lanes : (j + 1) * lanes]
        mask = jnp.where(row[:, None, :] == here, 1.0, mask)
    out_ref[...] = mask.reshape(out_ref.shape)


def chunk_kernel(*refs):
    own, others = refs[:4], refs[4:8]
    cot_ref, momentum_ref, mask_ref, table = refs[8:12]
    new_ref, kept_ref, lhs = refs[-3:]
    for shift in range(4):
        lhs[pl.ds(shift * 512, 128), :] = own[shift][...]
        lhs[pl.ds(shift * 512 + 128, 384), :] = others[shift][...]
    gradient = lax.dot_general(
        lhs[...], cot_ref[...], (((0,), (0,)), ((), ())), preferred_element_type=jnp.float32
    )
    blended = DECAY * momentum_ref[...] + gradient
    kept = forward(blended, table) * mask_ref[...]
    kept_ref[...] = kept
    new_ref[...] = blended - backward(kept, table)


def chunk(first, steps, own, others, cot, momentum, mask, table, previous, *before):
    rows, cols = momentum.shape
    low_rows, low_cols = TILE // SPAN * LOW, cols // SPAN * LOW
    in_specs = [pl.BlockSpec((128, TILE), lambda i: (0, first + i))] * 4
    in_specs += [pl.BlockSpec((384, TILE), lambda i: (0, i))] * 4
    in_specs += [
        pl.BlockSpec(cot.shape, lambda i: (0, 0)),
        pl.BlockSpec((TILE, cols), lambda i: (first + i, 0)),
        pl.BlockSpec((low_rows, low_cols), lambda i: (first + i, 0)),
        pl.BlockSpec(table.shape, lambda i: (0, 0)),
    ]
    args = [*own, *others, cot, momentum, mask, table, *before]
    aliases = {}
    if previous is not None:
        aliases = {len(args): 0}
        args.append(previous)
    return pl.pallas_call(
        chunk_kernel,
        grid=(steps,),
        in_specs=in_specs + [HBM] * (len(args) - 12),
        out_specs=[
            pl.BlockSpec((TILE, cols), lambda i: (first + i, 0)),
            pl.BlockSpec((low_rows, low_cols), lambda i: (i, 0)),
        ],
        out_shape=[
            jax.ShapeDtypeStruct((rows, cols), jnp.float32),
            jax.ShapeDtypeStruct((steps * low_rows, low_cols), jnp.float32),
        ],
        scratch_shapes=[pltpu.VMEM((2048, TILE), jnp.bfloat16)],
        input_output_aliases=aliases,
        compiler_params=PARAMS,
        cost_estimate=pl.CostEstimate(
            flops=2 * 2048 * TILE * cols * 2 * steps, bytes_accessed=steps * 3 * 2**20, transcendentals=0
        ),
        name=f"chunk{first}",
    )(*args)


def spread_kernel(first, steps, coefficients_ref, table, *refs):
    out_ref, made, sems = refs[-3:]
    low_rows = TILE // SPAN * LOW
    copies = []
    for i in range(steps):
        part = coefficients_ref[pl.ds(i * low_rows, low_rows), :]
        made[i] = backward(part, table).astype(made.dtype)
        rows = pl.ds((first + i) * TILE, TILE)
        copies.append(pltpu.make_async_copy(made.at[i], out_ref.at[rows, :], sems.at[i]))
        copies[-1].start()
    for copy in copies:
        copy.wait()


def spread(coefficients, shape, table):
    rows, cols = shape
    steps = rows // TILE
    return pl.pallas_call(
        lambda *refs: spread_kernel(0, steps, *refs),
        in_specs=[VMEM] * 2,
        out_specs=HBM,
        out_shape=jax.ShapeDtypeStruct(shape, jnp.bfloat16),
        scratch_shapes=[pltpu.VMEM((steps, TILE, cols), jnp.bfloat16), pltpu.SemaphoreType.DMA((steps,))],
        compiler_params=PARAMS,
        cost_estimate=pl.CostEstimate(flops=steps * 10**8, bytes_accessed=steps * 2**18, transcendentals=0),
        name="spread",
    )(coefficients, table)


def pack_kernel(*refs, start, places):
    out, held, loads, stores = refs[-4:]
    rows, width = refs[0].shape[0], out.shape[1]
    coming, going = [], []
    for i in range(places):
        here = held.at[pl.ds(i * rows, rows), :]
        coming.append(pltpu.make_async_copy(refs[i].at[:, pl.ds(start, width)], here, loads.at[i]))
        going.append(pltpu.make_async_copy(here, out.at[pl.ds(i * rows, rows), :], stores.at[i]))
        coming[-1].start()
    for i in range(places):
        coming[i].wait()
        going[i].start()
    for i in range(places):
        going[i].wait()


def pack(parts, start, width, *before):
    places, rows = len(parts), parts[0].shape[0]
    return pl.pallas_call(
        functools.partial(pack_kernel, start=start, places=places),
        in_specs=[HBM] * (places + len(before)),
        out_specs=HBM,
        out_shape=jax.ShapeDtypeStruct((places * rows, width), parts[0].dtype),
        scratch_shapes=[
            pltpu.VMEM((places * rows, width), parts[0].dtype),
            pltpu.SemaphoreType.DMA((places,)),
            pltpu.SemaphoreType.DMA((places,)),
        ],
        compiler_params=PARAMS,
        name="pack",
    )(*parts, *before)


def after(x, *before):
    return pl.pallas_call(
        lambda *refs: None,
        in_specs=[HBM] * (1 + len(before)),
        out_specs=HBM,
        out_shape=jax.ShapeDtypeStruct(x.shape, x.dtype),
        input_output_aliases={0: 0},
        compiler_params=PARAMS,
        name="after",
    )(x, *before)


def apart(x, axis, by):
    pairs = []
    for replica in range(16):
        step = by if replica % 2 == 0 else -by
        pairs += [(replica * 4 + i, replica * 4 + (i + step) % 4) for i in range(4)]
    return lax.ppermute(x, ("replica", axis), pairs)


def around(x, axis, mirrored=False):
    one = apart(x, axis, 1)
    three = apart(x, axis, -1)
    two = apart(three, axis, -1) if mirrored else apart(one, axis, 1)
    return [x, one, two, three]


def swapped(x, partner):
    pairs = []
    for i in range(16):
        z, core = partner(i // 2, i % 2)
        pairs.append((i, z * 2 + core))
    return lax.ppermute(x, "replica", pairs)


def halve_kernel(core_ref, *refs):
    parts, mine, theirs = refs[:-2], refs[-2], refs[-1]
    half, start = mine.shape[0], 0
    for part in parts:
        for row in range(0, part.shape[0], 64):
            upper = (start + row) // half
            value = part[pl.ds(row, 64), :]
            here = pl.ds((start + row) % half, 64)

            @pl.when(core_ref[0] == upper)
            def _():
                mine[here, :] = value

            @pl.when(core_ref[0] != upper)
            def _():
                theirs[here, :] = value

        start += part.shape[0]


def over_replicas(parts, core):
    half = jax.ShapeDtypeStruct((sum(p.shape[0] for p in parts) // 2, parts[0].shape[1]), parts[0].dtype)
    mine, theirs = pl.pallas_call(
        halve_kernel,
        in_specs=[SMEM] + [VMEM] * len(parts),
        out_specs=[VMEM] * 2,
        out_shape=[half, half],
        compiler_params=PARAMS,
        name="halve",
    )(core.reshape(1).astype(jnp.int32), *parts)
    mine = mine + swapped(theirs, lambda z, c: (z, 1 - c))
    def quad(z, c):
        return (((z - 2 * c) % 8 ^ 2) + 2 * c) % 8, c

    for partner in (lambda z, c: (z ^ 1, c), quad, lambda z, c: ((7 + 4 * c - z) % 8, c)):
        mine = mine + swapped(mine, partner)
    other = swapped(mine, lambda z, c: (z, 1 - c))
    return jnp.where(core == 0, jnp.concatenate([mine, other], 0), jnp.concatenate([other, mine], 0))


def pick_table(span_cols, band):
    pick = np.zeros((span_cols, band, band, span_cols, LOW), np.float32)
    for b in range(span_cols):
        for j in range(band):
            pick[b, j, j, b, :] = 1.0
    return pick.reshape(span_cols * band, band * span_cols * LOW).astype(ml_dtypes.bfloat16)


def local(activations, cotangent, momentum, band_index):
    momentum, band_index = momentum[0], band_index[0]
    rows, cols = momentum.shape
    span_rows, span_cols, band = band_index.shape
    fsdp = lax.axis_index("fsdp")
    tensor = lax.axis_index("tensor")
    core = lax.rem(lax.axis_index("replica"), 2)
    sign = 1 - 2 * core
    table = jnp.asarray(tables(cols))

    def columns(d, start, width):
        owner = lax.rem(fsdp + 4 + sign * d, 4)
        return lax.dynamic_slice(activations, (0, owner * rows + start), (activations.shape[0], width))

    mine = columns(0, 0, rows)
    own = around(mine, "tensor")
    pieces = [columns(d, 0, 1024) for d in (1, 2, 3)] + [columns(d, 1024, 1024) for d in (1, 2, 3)]
    early = [apart(pieces[d - 1], "fsdp", d) for d in (1, 2, 3)]
    late_one = apart(after(pieces[3], own[1], *early), "fsdp", 1)
    late_three = apart(after(pieces[5], own[1], *early), "fsdp", 3)
    late = [late_one, apart(after(pieces[4], late_one), "fsdp", 2), late_three]
    cots = around(pack([cotangent], 0, cols, late_one), "fsdp")

    chunks = [(0, 4), (4, 3), (7, 1)]
    units = [own]
    for first, steps in chunks:
        if first == 0:
            unit = pack(early, 0, 1024, own[1], own[3])
        else:
            before = [units[-1][1], units[-1][3]] if first == 4 else [own[2], units[-2][2], units[-1][1]]
            unit = pack(late, first * TILE - 1024, steps * TILE, *before)
        units.append(around(unit, "tensor", first in (0, 7)))
    others = units[1:]

    cot = pl.pallas_call(
        order_kernel,
        in_specs=[SMEM] + [VMEM] * 4,
        out_specs=VMEM,
        out_shape=jax.ShapeDtypeStruct((2048, cols), jnp.bfloat16),
        compiler_params=PARAMS,
        name="order",
    )(jnp.stack([tensor, sign]).astype(jnp.int32), *cots)

    mask = pl.pallas_call(
        mask_kernel,
        in_specs=[VMEM] * 2,
        out_specs=VMEM,
        out_shape=jax.ShapeDtypeStruct((span_rows * LOW, span_cols * LOW), jnp.float32),
        compiler_params=PARAMS,
        name="mask",
    )(band_index.transpose(1, 2, 0).reshape(span_cols * band, span_rows), jnp.asarray(pick_table(span_cols, band)))

    def part(i, previous, *before):
        first, steps = chunks[i]
        return chunk(first, steps, own, others[i], cot, momentum, mask, table, previous, *before)

    new_momentum, kept = None, []
    for i in range(len(chunks)):
        new_momentum, kept_i = part(i, new_momentum)
        kept.append(kept_i)
    combined = over_replicas(kept, core)
    update = spread(combined, (rows, cols), table)
    return (new_momentum[None], update)


def solution(mesh):
    in_specs = (
        P(("replica", "fsdp", "tensor"), None),
        P(("replica", "fsdp"), "tensor"),
        P("replica", "fsdp", "tensor"),
        P("replica", "fsdp", "tensor", None),
    )
    out_specs = (P("replica", "fsdp", "tensor"), P("fsdp", "tensor"))
    return jax.shard_map(local, mesh=mesh, in_specs=in_specs, out_specs=out_specs, check_vma=False)
```
